1024 devices in a mesh: node: 128 (over z, x, y_lo), local: 8 (over y_hi, core).
Axes of the slice: x: 4, y: 8 (y_hi: 4, y_lo: 2; y = y_hi * 2 + y_lo), z: 16, core: 2. Of those that a mesh axis runs over, the one named last changes fastest.
Arguments:
- tokens: bfloat16 [2048, 4096], P('local'), may hold values from -6 to 6
- codes: bfloat16 [4096, 14336], P(('local', 'node')), may hold values from -4 to 4
- scales: bfloat16 [4096, 128], P(('local', 'node')), may hold values from 0.0078125 to 0.03125
- cotangent: bfloat16 [2048, 14336], P('local', 'node'), may hold values from -6 to 6
Outputs:
- activated: bfloat16 [2048, 14336], P('local', 'node')
- grad_weight: bfloat16 [4096, 14336], P(('local', 'node'))
The draws below stay inside these ranges and needn't reach their ends.
All inputs are finite; a program needn't handle non-finite values.
Results may differ from the reference program's by a relative error of at most 0.0056.
Values may be sent and summed in bfloat16 or wider, within the bound.
A program may use at most 32 MiB of HBM per device.

```python
import math
import jax
import jax.numpy as jnp
from jax import lax

D = 4096
HW = 14336
BLK = 112
TOKENS = 2048


def strengthened(array, own_key, source, target, parts, factor):
    owner, partner = [(jnp.arange(array.shape[position]) // (array.shape[position] // parts)).reshape([-1 if axis == position else 1 for axis in range(array.ndim)]) for position in (source, target)]
    chosen = jax.random.permutation(own_key, parts)[partner]
    strong = (owner == chosen) | (owner == (partner + parts // 2) % parts)
    return jnp.where(strong, factor * array, array)


def shard_levels(key, shape, cuts, low, top_value):
    def one(position, parts):
        draws = jax.random.uniform(jax.random.fold_in(jax.random.fold_in(key, 6), position), (parts,), jnp.float32, low / len(cuts), top_value / len(cuts))
        return jnp.repeat(jnp.exp(draws), shape[position] // parts).reshape((-1,) + (1,) * (len(shape) - position - 1))

    factor_of = one(*cuts[0])
    for cut in cuts[1:]:
        factor_of = factor_of * one(*cut)
    return factor_of


def noise(stream_key, dims, width, bound, cuts=(), kind=jnp.bfloat16):
    values = jax.random.normal(stream_key, dims, jnp.float32) * width
    if len(cuts) > 0:
        values = shard_levels(stream_key, dims, cuts, -0.22, 0.18) * values
    return jnp.clip(values, min=-bound, max=bound).astype(kind)


def heavy_noise(own_key, dims, width, most, shards, heavy, held_as=jnp.bfloat16):
    drawn = width * jax.random.normal(own_key, dims, jnp.float32)
    if shards:
        drawn = drawn * shard_levels(own_key, dims, shards, -0.22, 0.18)
    return jnp.clip(strengthened(drawn, jax.random.fold_in(own_key, 3), *heavy), -most, most).astype(held_as)


def setup_inputs(seed: int = 0) -> dict:
    streams_of = jax.random.split(jax.random.key(seed), 5)
    return {
        "tokens": heavy_noise(streams_of[0], (TOKENS, D), 1.0, 6.0, ((0, 8),), (0, 1, 8, 2.0)),
        "codes": noise(streams_of[1], (D, HW), 1.0, 4.0, ((0, 1024),)),
        "scales": jnp.clip(jnp.exp(math.log(0.03125) - 1.3862944 * jax.random.uniform(streams_of[2], (D, HW // BLK), jnp.float32) ** shard_levels(streams_of[2], (D, HW // BLK), ((0, 1024),), -0.2, 0.2)), 0.0078125, 0.03125).astype(jnp.bfloat16),
        "cotangent": noise(streams_of[3], (TOKENS, HW), 1.0, 6.0, ((0, 8), (1, 128))),
    }


def restore(coded, block_scale):
    row_count, col_count = coded.shape
    grouped = coded.astype(jnp.float32).reshape(row_count, col_count // BLK, BLK)
    return (grouped * block_scale.astype(jnp.float32)[:, :, None]).reshape(row_count, col_count)


def reference(tokens, codes, scales, cotangent):
    weight = restore(codes, scales).astype(jnp.bfloat16)
    pre = jnp.dot(tokens, weight, preferred_element_type=jnp.float32)
    sig = jax.nn.sigmoid(pre)
    activated = (pre * sig).astype(jnp.bfloat16)
    grad_pre = (cotangent.astype(jnp.float32) * sig * (1.0 + pre * (1.0 - sig))).astype(jnp.bfloat16)
    factor = TOKENS ** -0.5
    summed = lax.dot_general(tokens, grad_pre, (((0,), (0,)), ((), ())), preferred_element_type=jnp.float32) * factor
    grad_weight = summed.astype(jnp.bfloat16)
    return activated, grad_weight
```

```python
import functools

import jax
import jax.numpy as jnp
from jax import lax
from jax.experimental import pallas as pl
from jax.experimental.pallas import tpu as pltpu
from jax.sharding import PartitionSpec as P

BLK = 112
MESH = pl.DeviceIdType.MESH
NZ, NXY, NY, NC = 16, 8, 4, 2
VMEM = pl.BlockSpec(memory_space=pltpu.VMEM)
F32, BF16 = jnp.float32, jnp.bfloat16


def kernel(
    rows, width, factor,
    tokens_hbm, codes, scales, cot_t,
    act_t, grad_out,
    tokens, wsend, wmid, wfull, pmine, psend, precv, ysend, yrecv, gblk, gmid, glast,
    tok_sem, own_sem, zs, zr, xs, xr, ys, yr, cs, cr,
    ps, pr, y2s, y2r, x2s, x2r, z2s, z2r,
):
    node, local = lax.axis_index("node"), lax.axis_index("local")
    z, xy, y, c = node // NXY, node % NXY, local // NC, local % NC
    block = NZ * NXY * rows
    partner = (node, y * NC + (1 - c))

    def at_z(other):
        return (other * NXY + xy, local)

    def at_xy(other):
        return (z * NXY + other, local)

    def at_y(other):
        return (node, other * NC + c)

    def send(src, dst, send_sem, recv_sem, device):
        copy = pltpu.make_async_remote_copy(
            src_ref=src, dst_ref=dst, send_sem=send_sem, recv_sem=recv_sem,
            device_id=device, device_id_type=MESH,
        )
        copy.start()
        return copy

    barrier = pltpu.get_barrier_semaphore()

    def greet(device):
        pl.semaphore_signal(barrier, inc=1, device_id=device, device_id_type=MESH)

    for d in range(1, NZ):
        greet(at_z((z + d) % NZ))
    for d in range(1, NXY):
        greet(at_xy((xy + d) % NXY))
    for d in range(1, NY):
        greet(at_y((y + d) % NY))
    greet(partner)

    tok_copy = pltpu.make_async_copy(tokens_hbm, tokens, tok_sem)
    tok_copy.start()

    scale = scales[...].astype(F32)
    for n in range(NZ * NXY):
        piece = codes[:, n * BLK:(n + 1) * BLK].astype(F32) * scale[:, n:n + 1]
        wsend[n // NXY, n % NXY] = piece.astype(BF16)

    pl.semaphore_wait(barrier, NZ - 1 + NXY - 1 + NY - 1 + 1)

    out = [
        send(wsend.at[(z + d) % NZ], wmid.at[z], zs.at[(z + d) % NZ], zr.at[z], at_z((z + d) % NZ))
        for d in range(1, NZ)
    ]
    own = pltpu.make_async_copy(wsend.at[z], wmid.at[z], own_sem.at[0])
    own.start()
    own.wait()
    for d in range(1, NZ):
        s = (z + d) % NZ
        pltpu.make_async_copy(wmid.at[s], wmid.at[s], zr.at[s]).wait()
    out += [
        send(wmid.at[:, (xy + d) % NXY], wfull.at[local, :, xy], xs.at[(xy + d) % NXY], xr.at[xy],
             at_xy((xy + d) % NXY))
        for d in range(1, NXY)
    ]
    own = pltpu.make_async_copy(wmid.at[:, xy], wfull.at[local, :, xy], own_sem.at[1])
    own.start()
    own.wait()
    for d in range(1, NXY):
        s = (xy + d) % NXY
        pltpu.make_async_copy(wfull.at[local, :, s], wfull.at[local, :, s], xr.at[s]).wait()

    out += [
        send(wfull.at[local], wfull.at[local], ys.at[(y + d) % NY], yr.at[y], at_y((y + d) % NY))
        for d in (2, 1, 3)
    ]
    out.append(send(wfull.at[local], wfull.at[local], cs.at[y], cr.at[y], partner))
    tok_copy.wait()

    def product(owner):
        start = pl.multiple_of(owner * block, block)
        return jnp.dot(
            tokens[:, pl.ds(start, block)], wfull[owner].reshape(block, BLK),
            preferred_element_type=F32,
        )

    pre = product(local)
    other = y * NC + 1 - c
    pltpu.make_async_copy(wfull.at[other], wfull.at[other], cr.at[y]).wait()
    pre += product(other)
    for d in (1, 3, 2):
        s = (y + d) % NY
        mine = s * NC + c
        pltpu.make_async_copy(wfull.at[mine], wfull.at[mine], yr.at[s]).wait()
        out.append(send(wfull.at[mine], wfull.at[mine], cs.at[s], cr.at[s], partner))
        pre += product(mine)
    for d in (1, 3, 2):
        s = (y + d) % NY
        other = s * NC + 1 - c
        pltpu.make_async_copy(wfull.at[other], wfull.at[other], cr.at[s]).wait()
        pre += product(other)

    sig = jax.nn.sigmoid(pre)
    act_t[...] = (pre * sig).T.astype(BF16)
    cot = cot_t[...].astype(F32).T
    grad_pre = (cot * sig * (1.0 + pre * (1.0 - sig))).astype(BF16)

    def term(owner):
        start = pl.multiple_of(owner * block, block)
        return lax.dot_general(
            tokens[:, pl.ds(start, block)], grad_pre, (((0,), (0,)), ((), ())),
            preferred_element_type=F32,
        )

    order = (2, 1, 3, 0)
    for d in order:
        s = (y + d) % NY
        psend[s] = term(s * NC + 1 - c)
        out.append(send(psend.at[s], precv.at[s], ps.at[s], pr.at[s], partner))
    for d in order:
        s = (y + d) % NY
        mine = term(s * NC + c)
        pltpu.make_async_copy(precv.at[s], precv.at[s], pr.at[s]).wait()
        mine = mine + precv[s]
        if d:
            ysend[s] = mine.astype(BF16)
            out.append(send(ysend.at[s], yrecv.at[y], y2s.at[s], y2r.at[y], at_y(s)))
        else:
            pmine[...] = mine
    total = pmine[...]
    for d in (1, 3, 2):
        s = (y + d) % NY
        pltpu.make_async_copy(yrecv.at[s], yrecv.at[s], y2r.at[s]).wait()
        total = total + yrecv[s].astype(F32)
    gblk[...] = (total * factor).astype(BF16).reshape(NZ, NXY, rows, BLK)

    out += [
        send(gblk.at[:, (xy + d) % NXY], gmid.at[:, xy], x2s.at[(xy + d) % NXY], x2r.at[xy],
             at_xy((xy + d) % NXY))
        for d in range(1, NXY)
    ]
    own = pltpu.make_async_copy(gblk.at[:, xy], gmid.at[:, xy], own_sem.at[2])
    own.start()
    own.wait()
    for d in range(1, NXY):
        s = (xy + d) % NXY
        pltpu.make_async_copy(gmid.at[:, s], gmid.at[:, s], x2r.at[s]).wait()
    out += [
        send(gmid.at[(z + d) % NZ], glast.at[z], z2s.at[(z + d) % NZ], z2r.at[z], at_z((z + d) % NZ))
        for d in range(1, NZ)
    ]
    own = pltpu.make_async_copy(gmid.at[z], glast.at[z], own_sem.at[3])
    own.start()
    own.wait()
    for d in range(1, NZ):
        s = (z + d) % NZ
        pltpu.make_async_copy(glast.at[s], glast.at[s], z2r.at[s]).wait()
    for n in range(NZ * NXY):
        grad_out[:, n * BLK:(n + 1) * BLK] = glast[n // NXY, n % NXY]
    for copy in out:
        copy.wait_send()


def body(tokens, codes, scales, cotangent):
    tok_rows, depth = tokens.shape
    rows, width = codes.shape
    block = NZ * NXY * rows
    factor = (tok_rows * NY * NC) ** (-0.5)
    piece = (NZ, NXY, rows, BLK)
    dma = pltpu.SemaphoreType.DMA
    act_t, grad = pl.pallas_call(
        functools.partial(kernel, rows, width, factor),
        out_shape=(
            jax.ShapeDtypeStruct((BLK, tok_rows), BF16),
            jax.ShapeDtypeStruct((rows, width), BF16),
        ),
        in_specs=[pl.BlockSpec(memory_space=pl.ANY), VMEM, VMEM, VMEM],
        out_specs=(VMEM, VMEM),
        scratch_shapes=[
            pltpu.VMEM((tok_rows, depth), BF16),
            pltpu.VMEM(piece, BF16),
            pltpu.VMEM(piece, BF16),
            pltpu.VMEM((NY * NC, *piece), BF16),
            pltpu.VMEM((block, BLK), F32),
            pltpu.VMEM((NY, block, BLK), F32),
            pltpu.VMEM((NY, block, BLK), F32),
            pltpu.VMEM((NY, block, BLK), BF16),
            pltpu.VMEM((NY, block, BLK), BF16),
            pltpu.VMEM(piece, BF16),
            pltpu.VMEM(piece, BF16),
            pltpu.VMEM(piece, BF16),
            dma, dma((4,)),
            dma((NZ,)), dma((NZ,)), dma((NXY,)), dma((NXY,)),
            dma((NY,)), dma((NY,)), dma((NY,)), dma((NY,)),
            dma((NY,)), dma((NY,)), dma((NY,)), dma((NY,)),
            dma((NXY,)), dma((NXY,)), dma((NZ,)), dma((NZ,)),
        ],
        compiler_params=pltpu.CompilerParams(
            collective_id=0, has_side_effects=True, vmem_limit_bytes=48 << 20
        ),
        cost_estimate=pl.CostEstimate(
            flops=4 * tok_rows * depth * BLK, bytes_accessed=4 << 20, transcendentals=tok_rows * BLK
        ),
    )(tokens, codes, scales, cotangent.T)
    return (act_t.T, grad)


def solution(mesh):
    placed = (
        P("local", None),
        P(("local", "node"), None),
        P(("local", "node"), None),
        P("local", "node"),
    )
    return jax.shard_map(
        body,
        mesh=mesh,
        in_specs=placed,
        out_specs=(P("local", "node"), P(("local", "node"), None)),
        check_vma=False,
    )
```

```python
import functools

import jax
import jax.numpy as jnp
from jax import lax
from jax.experimental import pallas as pl
from jax.experimental.pallas import tpu as pltpu
from jax.sharding import PartitionSpec as P

BLK = 112
MESH = pl.DeviceIdType.MESH
NZ, NXY, NY, NC = 16, 8, 4, 2
NQ = 4
FAR_FIRST = (8, 7, 9, 6, 10, 5, 11, 4, 12, 3, 13, 2, 14, 1, 15)
VMEM = pl.BlockSpec(memory_space=pltpu.VMEM)
F32, BF16 = jnp.float32, jnp.bfloat16


def kernel(
    rows, factor,
    tokens_hbm, codes_hbm, scales_hbm, cot_hbm,
    act_t, grad_out,
    tokens, codes, scales, cot_t,
    wsend, wmid, wfull, pmine, psend, precv, ysend, yrecv, gblk, gmid, glast,
    in_sem, own_sem, zs, zr, xs, xr, ys, yr, cs, cr,
    ps, pr, y2s, y2r, x2s, x2r, z2s, z2r,
):
    node, local = lax.axis_index("node"), lax.axis_index("local")
    z, xy, y, c = node // NXY, node % NXY, local // NC, local % NC
    zq, zi = z // NQ, z % NQ
    part = NQ * NXY * rows
    block = NQ * part
    partner = (node, y * NC + (1 - c))

    def at_z(other):
        return (other * NXY + xy, local)

    def at_xy(other):
        return (z * NXY + other, local)

    def at_y(other):
        return (node, other * NC + c)

    out = []

    def send(src, dst, send_sem, recv_sem, device):
        copy = pltpu.make_async_remote_copy(
            src_ref=src, dst_ref=dst, send_sem=send_sem, recv_sem=recv_sem,
            device_id=device, device_id_type=MESH,
        )
        copy.start()
        out.append(copy)

    def landed(ref, sem):
        pltpu.make_async_copy(ref, ref, sem).wait()

    barrier = pltpu.get_barrier_semaphore()

    def greet(device):
        pl.semaphore_signal(barrier, inc=1, device_id=device, device_id_type=MESH)

    for d in FAR_FIRST:
        greet(at_z((z + d) % NZ))
    for d in range(1, NXY):
        greet(at_xy((xy + d) % NXY))
    for d in range(1, NY):
        greet(at_y((y + d) % NY))
    greet(partner)

    loads = [
        pltpu.make_async_copy(src, dst, in_sem.at[i])
        for i, (src, dst) in enumerate(
            ((codes_hbm, codes), (scales_hbm, scales), (tokens_hbm, tokens), (cot_hbm, cot_t))
        )
    ]
    for load in loads:
        load.start()
    loads[0].wait()
    loads[1].wait()

    scale = scales[...].astype(F32)
    for n in range(NZ * NXY):
        piece = codes[:, n * BLK:(n + 1) * BLK].astype(F32) * scale[:, n:n + 1]
        wsend[n // NXY, n % NXY] = piece.astype(BF16)

    pl.semaphore_wait(barrier, NZ - 1 + NXY - 1 + NY - 1 + 1)

    for d in FAR_FIRST:
        t = (z + d) % NZ
        send(wsend.at[t], wmid.at[z], zs.at[t], zr.at[z], at_z(t))
    own_z = pltpu.make_async_copy(wsend.at[z], wmid.at[z], own_sem.at[0])
    own_z.start()
    own_z.wait()

    def quarter(step):
        return (zq + step) % NQ

    def zs_of(q):
        return pl.ds(q * NQ, NQ)

    def over_xy(step):
        q = quarter(step)
        for i in range(NQ):
            if step:
                landed(wmid.at[q * NQ + i], zr.at[q * NQ + i])
            elif i:
                t = q * NQ + (zi + i) % NQ
                landed(wmid.at[t], zr.at[t])
        for d in range(1, NXY):
            t = (xy + d) % NXY
            send(wmid.at[zs_of(q), t], wfull.at[local, zs_of(q), xy], xs.at[q, t], xr.at[q, xy], at_xy(t))
        own = pltpu.make_async_copy(wmid.at[zs_of(q), xy], wfull.at[local, zs_of(q), xy], own_sem.at[1 + step])
        own.start()
        return own

    def over_y(step, own):
        q = quarter(step)
        own.wait()
        for d in range(1, NXY):
            t = (xy + d) % NXY
            landed(wfull.at[local, zs_of(q), t], xr.at[q, t])
        here = wfull.at[local, zs_of(q)]
        for d in (2, 1, 3):
            t = (y + d) % NY
            send(here, here, ys.at[q, t], yr.at[q, y], at_y(t))
        send(here, here, cs.at[q, y], cr.at[q, y], partner)

    fwd = (0, 1, 3, 2)
    last = None
    for step in fwd:
        own = over_xy(step)
        if last is not None:
            over_y(*last)
        last = (step, own)
    over_y(*last)
    loads[2].wait()
    loads[3].wait()

    def product(owner, q):
        start = pl.multiple_of(owner * block + q * part, part)
        return jnp.dot(
            tokens[:, pl.ds(start, part)], wfull[owner, zs_of(q)].reshape(part, BLK),
            preferred_element_type=F32,
        )

    pre = jnp.zeros((tokens.shape[0], BLK), F32)
    for step in fwd:
        q = quarter(step)
        for d in (1, 3, 2):
            s = (y + d) % NY
            here = wfull.at[s * NC + c, zs_of(q)]
            landed(here, yr.at[q, s])
            send(here, here, cs.at[q, s], cr.at[q, s], partner)
        for d in range(NY):
            pre += product((y + d) % NY * NC + c, q)
        for d in range(NY):
            s = (y + d) % NY
            other = s * NC + 1 - c
            landed(wfull.at[other, zs_of(q)], cr.at[q, s])
            pre += product(other, q)

    sig = jax.nn.sigmoid(pre)
    cot = cot_t[...].astype(F32).T
    grad_pre = (cot * sig * (1.0 + pre * (1.0 - sig))).astype(BF16)

    def term(owner, q):
        start = pl.multiple_of(owner * block + q * part, part)
        return lax.dot_general(
            tokens[:, pl.ds(start, part)], grad_pre, (((0,), (0,)), ((), ())),
            preferred_element_type=F32,
        )

    bwd = (2, 1, 3, 0)
    for step in bwd:
        q = quarter(step)
        for s in range(NY):
            psend[q, s] = term(s * NC + 1 - c, q)
        send(psend.at[q], precv.at[q], ps.at[q], pr.at[q], partner)
    for step in bwd:
        q = quarter(step)
        mine = [term((y + d) % NY * NC + c, q) for d in range(NY)]
        landed(precv.at[q], pr.at[q])
        for d in (2, 1, 3, 0):
            s = (y + d) % NY
            both = mine[d] + precv[q, s]
            if d:
                ysend[q, s] = both.astype(BF16)
                send(ysend.at[q, s], yrecv.at[q, y], y2s.at[q, s], y2r.at[q, y], at_y(s))
            else:
                pmine[q] = both
    act_t[...] = (pre * sig).T.astype(BF16)

    def back_xy(step):
        q = quarter(step)
        total = pmine[q]
        for d in (1, 3, 2):
            s = (y + d) % NY
            landed(yrecv.at[q, s], y2r.at[q, s])
            total = total + yrecv[q, s].astype(F32)
        gblk[zs_of(q)] = (total * factor).astype(BF16).reshape(NQ, NXY, rows, BLK)
        for d in range(1, NXY):
            t = (xy + d) % NXY
            send(gblk.at[zs_of(q), t], gmid.at[zs_of(q), xy], x2s.at[q, t], x2r.at[q, xy], at_xy(t))
        own = pltpu.make_async_copy(gblk.at[zs_of(q), xy], gmid.at[zs_of(q), xy], own_sem.at[5 + step])
        own.start()
        return own

    def back_z(step, own):
        q = quarter(step)
        own.wait()
        for d in range(1, NXY):
            s = (xy + d) % NXY
            landed(gmid.at[zs_of(q), s], x2r.at[q, s])
        for i in range(NQ):
            t = q * NQ + (i if step else (zi + i) % NQ)
            if step or i:
                send(gmid.at[t], glast.at[z], z2s.at[t], z2r.at[z], at_z(t))
        if step == 0:
            home = pltpu.make_async_copy(gmid.at[z], glast.at[z], own_sem.at[9])
            home.start()
            home.wait()

    last = None
    for step in bwd:
        own = back_xy(step)
        if last is not None:
            back_z(*last)
        last = (step, own)
    back_z(*last)
    for d in FAR_FIRST:
        s = (z + d) % NZ
        landed(glast.at[s], z2r.at[s])
    for n in range(NZ * NXY):
        grad_out[:, n * BLK:(n + 1) * BLK] = glast[n // NXY, n % NXY]
    for copy in out:
        copy.wait_send()


def body(tokens, codes, scales, cotangent):
    tok_rows, depth = tokens.shape
    rows, width = codes.shape
    part = NQ * NXY * rows
    factor = (tok_rows * NY * NC) ** (-0.5)
    piece = (NZ, NXY, rows, BLK)
    dma = pltpu.SemaphoreType.DMA
    act_t, grad = pl.pallas_call(
        functools.partial(kernel, rows, factor),
        out_shape=(
            jax.ShapeDtypeStruct((BLK, tok_rows), BF16),
            jax.ShapeDtypeStruct((rows, width), BF16),
        ),
        in_specs=[pl.BlockSpec(memory_space=pl.ANY)] * 4,
        out_specs=(VMEM, VMEM),
        scratch_shapes=[
            pltpu.VMEM((tok_rows, depth), BF16),
            pltpu.VMEM((rows, width), BF16),
            pltpu.VMEM(scales.shape, BF16),
            pltpu.VMEM((BLK, tok_rows), BF16),
            pltpu.VMEM(piece, BF16),
            pltpu.VMEM(piece, BF16),
            pltpu.VMEM((NY * NC, *piece), BF16),
            pltpu.VMEM((NQ, part, BLK), F32),
            pltpu.VMEM((NQ, NY, part, BLK), F32),
            pltpu.VMEM((NQ, NY, part, BLK), F32),
            pltpu.VMEM((NQ, NY, part, BLK), BF16),
            pltpu.VMEM((NQ, NY, part, BLK), BF16),
            pltpu.VMEM(piece, BF16),
            pltpu.VMEM(piece, BF16),
            pltpu.VMEM(piece, BF16),
            dma((4,)), dma((10,)),
            dma((NZ,)), dma((NZ,)), dma((NQ, NXY)), dma((NQ, NXY)),
            dma((NQ, NY)), dma((NQ, NY)), dma((NQ, NY)), dma((NQ, NY)),
            dma((NQ,)), dma((NQ,)), dma((NQ, NY)), dma((NQ, NY)),
            dma((NQ, NXY)), dma((NQ, NXY)), dma((NZ,)), dma((NZ,)),
        ],
        compiler_params=pltpu.CompilerParams(
            collective_id=0, has_side_effects=True, vmem_limit_bytes=62 << 20
        ),
        cost_estimate=pl.CostEstimate(
            flops=4 * tok_rows * depth * BLK, bytes_accessed=4 << 20, transcendentals=tok_rows * BLK
        ),
    )(tokens, codes, scales, cotangent.T)
    return (act_t.T, grad)


def solution(mesh):
    placed = (
        P("local", None),
        P(("local", "node"), None),
        P(("local", "node"), None),
        P("local", "node"),
    )
    return jax.shard_map(
        body,
        mesh=mesh,
        in_specs=placed,
        out_specs=(P("local", "node"), P(("local", "node"), None)),
        check_vma=False,
    )
```

```python
import functools

import jax
import jax.numpy as jnp
from jax import lax
from jax.experimental import pallas as pl
from jax.experimental.pallas import tpu as pltpu
from jax.sharding import PartitionSpec as P

BLK = 112
MESH = pl.DeviceIdType.MESH
NZ, NXY, NY, NC = 16, 8, 4, 2
NQ = 4
NEAR_FIRST = (1, 15, 2, 14, 3, 13, 4, 12, 5, 11, 6, 10, 7, 9, 8)
NEAR_QUARTERS, FAR_QUARTERS = (0, 1, 3, 2), (2, 1, 3, 0)
VMEM = pl.BlockSpec(memory_space=pltpu.VMEM)
F32, BF16 = jnp.float32, jnp.bfloat16


def kernel(
    rows, factor,
    tokens_hbm, codes_hbm, scales_hbm, cot_hbm,
    act_t, grad_out,
    tokens, codes, scales, cot_t,
    wsend, wmid, wfull, psend, precv, ysend, yrecv, gmid, glast,
    in_sem, own_sem, zs, zr, ys, yr, cs, cr,
    ps, pr, y2s, y2r, z2s, z2r,
):
    node, local = lax.axis_index("node"), lax.axis_index("local")
    z, xy, y, c = node // NXY, node % NXY, local // NC, local % NC
    zq, zi = z // NQ, z % NQ
    part = NQ * NXY * rows
    block = NQ * part
    partner = (node, y * NC + (1 - c))

    def at_z(other):
        return (other * NXY + xy, local)

    def at_plane(other_xy, other_y):
        return (z * NXY + other_xy, other_y * NC + c)

    def remote(src, dst, send_sem, recv_sem, device):
        return pltpu.make_async_remote_copy(
            src_ref=src, dst_ref=dst, send_sem=send_sem, recv_sem=recv_sem,
            device_id=device, device_id_type=MESH,
        )

    def landed(ref, sem):
        pltpu.make_async_copy(ref, ref, sem).wait()

    def plane(visit):
        for dy in (2, 1, 3, 0):
            @pl.loop(0 if dy else 1, NXY)
            def _(dx):
                visit((xy + dx) % NXY, (y + dy) % NY)

    barrier = pltpu.get_barrier_semaphore()

    def greet(device):
        pl.semaphore_signal(barrier, inc=1, device_id=device, device_id_type=MESH)

    for d in NEAR_FIRST[::-1]:
        greet(at_z((z + d) % NZ))
    plane(lambda t_xy, t_y: greet(at_plane(t_xy, t_y)))
    greet(partner)

    loads = [
        pltpu.make_async_copy(src, dst, in_sem.at[i])
        for i, (src, dst) in enumerate(
            ((codes_hbm, codes), (scales_hbm, scales), (tokens_hbm, tokens), (cot_hbm, cot_t))
        )
    ]
    for load in loads:
        load.start()
    loads[0].wait()
    loads[1].wait()

    scale = scales[...].astype(F32)
    for n in range(NZ * NXY):
        piece = codes[:, n * BLK:(n + 1) * BLK].astype(F32) * scale[:, n:n + 1]
        wsend[n // NXY, n % NXY] = piece.astype(BF16)

    pl.semaphore_wait(barrier, NZ - 1 + NXY * NY - 1 + 1)

    def z_copy(d):
        t = (z + d) % NZ
        return remote(wsend.at[t], wmid.at[z], zs.at[t], zr.at[z], at_z(t))

    for d in NEAR_FIRST:
        z_copy(d).start()
    own_z = pltpu.make_async_copy(wsend.at[z], wmid.at[z], own_sem.at[0])
    own_z.start()
    own_z.wait()

    def zs_of(q):
        return pl.ds(q * NQ, NQ)

    def plane_copy(q, t_xy, t_y):
        return remote(
            wmid.at[zs_of(q), t_xy], wfull.at[local, zs_of(q), xy],
            ys.at[q, t_y, t_xy], yr.at[q, y, xy], at_plane(t_xy, t_y),
        )

    def own_copy(step, q):
        return pltpu.make_async_copy(
            wmid.at[zs_of(q), xy], wfull.at[local, zs_of(q), xy], own_sem.at[1 + step]
        )

    for step in NEAR_QUARTERS:
        q = (zq + step) % NQ
        for i in range(NQ):
            s = q * NQ + (i if step else (zi + i) % NQ)
            if step or i:
                landed(wmid.at[s], zr.at[s])
        plane(lambda t_xy, t_y: plane_copy(q, t_xy, t_y).start())
        own_copy(step, q).start()
    loads[2].wait()
    loads[3].wait()

    def core_copy(q, s):
        here = wfull.at[s * NC + c, zs_of(q)]
        return remote(here, here, cs.at[q, s], cr.at[q, s], partner)

    def product(owner, q):
        start = pl.multiple_of(owner * block + q * part, part)
        return jnp.dot(
            tokens[:, pl.ds(start, part)], wfull[owner, zs_of(q)].reshape(part, BLK),
            preferred_element_type=F32,
        )

    pre = jnp.zeros((tokens.shape[0], BLK), F32)
    for step in NEAR_QUARTERS:
        q = (zq + step) % NQ
        for d in (0, 1, 3, 2):
            s = (y + d) % NY
            mine = s * NC + c

            @pl.loop(0 if d else 1, NXY)
            def _(dx):
                t = (xy + dx) % NXY
                landed(wfull.at[mine, zs_of(q), t], yr.at[q, s, t])

            if d == 0:
                own_copy(step, q).wait()
            core_copy(q, s).start()
            pre += product(mine, q)
        for d in (0, 1, 3, 2):
            s = (y + d) % NY
            other = s * NC + 1 - c
            landed(wfull.at[other, zs_of(q)], cr.at[q, s])
            pre += product(other, q)

    sig = jax.nn.sigmoid(pre)
    cot = cot_t[...].astype(F32).T
    grad_pre = (cot * sig * (1.0 + pre * (1.0 - sig))).astype(BF16)

    def term(owner, q):
        start = pl.multiple_of(owner * block + q * part, part)
        return lax.dot_general(
            tokens[:, pl.ds(start, part)], grad_pre, (((0,), (0,)), ((), ())),
            preferred_element_type=F32,
        )

    def pair_copy(q):
        return remote(psend.at[q], precv.at[q], ps.at[q], pr.at[q], partner)

    def back_copy(q, t_xy, t_y):
        return remote(
            ysend.at[q, t_y, :, t_xy], yrecv.at[q, y, :, xy],
            y2s.at[q, t_y, t_xy], y2r.at[q, y, xy], at_plane(t_xy, t_y),
        )

    def own_back(step, q):
        return pltpu.make_async_copy(ysend.at[q, y, :, xy], yrecv.at[q, y, :, xy], own_sem.at[5 + step])

    for step in FAR_QUARTERS:
        q = (zq + step) % NQ
        for s in range(NY):
            psend[q, s] = term(s * NC + 1 - c, q)
        pair_copy(q).start()
    for step in FAR_QUARTERS:
        q = (zq + step) % NQ
        mine = [term(s * NC + c, q) for s in range(NY)]
        landed(precv.at[q], pr.at[q])
        for s in range(NY):
            ysend[q, s] = (mine[s] + precv[q, s]).astype(BF16).reshape(NQ, NXY, rows, BLK)
        plane(lambda t_xy, t_y: back_copy(q, t_xy, t_y).start())
        own_back(step, q).start()
    act_t[...] = (pre * sig).T.astype(BF16)

    for d in NEAR_FIRST:
        z_copy(d).wait_send()
    for q in range(NQ):
        plane(lambda t_xy, t_y: plane_copy(q, t_xy, t_y).wait_send())
        for s in range(NY):
            core_copy(q, s).wait_send()
        pair_copy(q).wait_send()

    def home_copy(t):
        return remote(gmid.at[t], glast.at[z], z2s.at[t], z2r.at[z], at_z(t))

    for step in FAR_QUARTERS:
        q = (zq + step) % NQ
        own_back(step, q).wait()
        total = None
        for d in (0, 1, 3, 2):
            s = (y + d) % NY

            @pl.loop(0 if d else 1, NXY)
            def _(dx):
                t = (xy + dx) % NXY
                landed(yrecv.at[q, s, :, t], y2r.at[q, s, t])

            term_here = yrecv[q, s].reshape(part, BLK).astype(F32)
            total = term_here if total is None else total + term_here
        gmid[zs_of(q)] = (total * factor).astype(BF16).reshape(NQ, NXY, rows, BLK)
        for i in range(NQ):
            t = q * NQ + (i if step else (zi + i) % NQ)
            if step or i:
                home_copy(t).start()
    home = pltpu.make_async_copy(gmid.at[z], glast.at[z], own_sem.at[9])
    home.start()
    for q in range(NQ):
        plane(lambda t_xy, t_y: back_copy(q, t_xy, t_y).wait_send())
    home.wait()
    for d in NEAR_FIRST:
        s = (z + d) % NZ
        landed(glast.at[s], z2r.at[s])
    for n in range(NZ * NXY):
        grad_out[:, n * BLK:(n + 1) * BLK] = glast[n // NXY, n % NXY]
    for d in NEAR_FIRST:
        home_copy((z + d) % NZ).wait_send()


def body(tokens, codes, scales, cotangent):
    tok_rows, depth = tokens.shape
    rows, width = codes.shape
    part = NQ * NXY * rows
    factor = (tok_rows * NY * NC) ** (-0.5)
    piece = (NZ, NXY, rows, BLK)
    dma = pltpu.SemaphoreType.DMA
    act_t, grad = pl.pallas_call(
        functools.partial(kernel, rows, factor),
        out_shape=(
            jax.ShapeDtypeStruct((BLK, tok_rows), BF16),
            jax.ShapeDtypeStruct((rows, width), BF16),
        ),
        in_specs=[pl.BlockSpec(memory_space=pl.ANY)] * 4,
        out_specs=(VMEM, VMEM),
        scratch_shapes=[
            pltpu.VMEM((tok_rows, depth), BF16),
            pltpu.VMEM((rows, width), BF16),
            pltpu.VMEM(scales.shape, BF16),
            pltpu.VMEM((BLK, tok_rows), BF16),
            pltpu.VMEM(piece, BF16),
            pltpu.VMEM(piece, BF16),
            pltpu.VMEM((NY * NC, *piece), BF16),
            pltpu.VMEM((NQ, NY, part, BLK), F32),
            pltpu.VMEM((NQ, NY, part, BLK), F32),
            pltpu.VMEM((NQ, NY, NQ, NXY, rows, BLK), BF16),
            pltpu.VMEM((NQ, NY, NQ, NXY, rows, BLK), BF16),
            pltpu.VMEM(piece, BF16),
            pltpu.VMEM(piece, BF16),
            dma((4,)), dma((10,)), dma((NZ,)), dma((NZ,)),
            dma((NQ, NY, NXY)), dma((NQ, NY, NXY)), dma((NQ, NY)), dma((NQ, NY)),
            dma((NQ,)), dma((NQ,)), dma((NQ, NY, NXY)), dma((NQ, NY, NXY)), dma((NZ,)), dma((NZ,)),
        ],
        compiler_params=pltpu.CompilerParams(
            collective_id=0, has_side_effects=True, vmem_limit_bytes=62 << 20
        ),
        cost_estimate=pl.CostEstimate(
            flops=4 * tok_rows * depth * BLK, bytes_accessed=4 << 20, transcendentals=tok_rows * BLK
        ),
    )(tokens, codes, scales, cotangent.T)
    return (act_t.T, grad)


def solution(mesh):
    placed = (
        P("local", None),
        P(("local", "node"), None),
        P(("local", "node"), None),
        P("local", "node"),
    )
    return jax.shard_map(
        body,
        mesh=mesh,
        in_specs=placed,
        out_specs=(P("local", "node"), P(("local", "node"), None)),
        check_vma=False,
    )
```

```python
import functools

import jax
import jax.numpy as jnp
from jax import lax
from jax.experimental import pallas as pl
from jax.experimental.pallas import tpu as pltpu
from jax.sharding import PartitionSpec as P

BLK = 112
MESH = pl.DeviceIdType.MESH
NZ, NXY, NY, NC = 16, 8, 4, 2
NQ = 4
NEAR_FIRST = (1, 15, 2, 14, 3, 13, 4, 12, 5, 11, 6, 10, 7, 9, 8)
NEAR_QUARTERS, FAR_QUARTERS = (0, 1, 3, 2), (2, 1, 3, 0)
VMEM = pl.BlockSpec(memory_space=pltpu.VMEM)
F32, BF16 = jnp.float32, jnp.bfloat16


def kernel(
    rows, factor,
    tokens_hbm, codes_hbm, scales_hbm, cot_hbm,
    act_hbm, glast,
    tokens, codes, scales, cot_t, act_t,
    wsend, wmid, wfull, psend, precv, ysend, yrecv, gmid,
    in_sem, act_sem, zs, zr, ys, yr, cs, cr,
    ps, pr, y2s, y2r, z2s, z2r,
):
    node, local = lax.axis_index("node"), lax.axis_index("local")
    z, xy, y, c = node // NXY, node % NXY, local // NC, local % NC
    zq, zi = z // NQ, z % NQ
    part = NQ * NXY * rows
    block = NQ * part
    partner = (node, y * NC + (1 - c))

    def at_z(other):
        return (other * NXY + xy, local)

    def at_plane(other_xy, other_y):
        return (z * NXY + other_xy, other_y * NC + c)

    def remote(src, dst, send_sem, recv_sem, device):
        return pltpu.make_async_remote_copy(
            src_ref=src, dst_ref=dst, send_sem=send_sem, recv_sem=recv_sem,
            device_id=device, device_id_type=MESH,
        )

    def landed(ref, sem):
        pltpu.make_async_copy(ref, ref, sem).wait()

    def plane(visit):
        for dy in (2, 1, 3, 0):
            @pl.loop(0 if dy else 1, NXY)
            def _(dx):
                visit((xy + dx) % NXY, (y + dy) % NY)

    loads = [
        pltpu.make_async_copy(src, dst, in_sem.at[i])
        for i, (src, dst) in enumerate(
            ((codes_hbm, codes), (scales_hbm, scales), (tokens_hbm, tokens), (cot_hbm, cot_t))
        )
    ]
    for load in loads:
        load.start()

    barrier = pltpu.get_barrier_semaphore()

    def greet(device):
        pl.semaphore_signal(barrier, inc=1, device_id=device, device_id_type=MESH)

    for d in NEAR_FIRST[::-1]:
        greet(at_z((z + d) % NZ))
    plane(lambda t_xy, t_y: greet(at_plane(t_xy, t_y)))
    greet(partner)

    loads[0].wait()
    loads[1].wait()

    scale = scales[...].astype(F32)
    for n in range(NZ * NXY):
        piece = codes[:, n * BLK:(n + 1) * BLK].astype(F32) * scale[:, n:n + 1]
        wsend[n // NXY, n % NXY] = piece.astype(BF16)

    pl.semaphore_wait(barrier, NZ - 1 + NXY * NY - 1 + 1)

    def z_copy(d):
        t = (z + d) % NZ
        return remote(wsend.at[t], wmid.at[z], zs, zr.at[zq], at_z(t))

    for d in NEAR_FIRST:
        z_copy(d).start()
    pltpu.make_async_copy(wsend.at[z], wmid.at[z], zr.at[zq]).start()

    def zs_of(q):
        return pl.ds(q * NQ, NQ)

    def full_of(owner, q):
        return pl.ds(owner * NZ + q * NQ, NQ)

    def plane_copy(q, t_xy, t_y):
        return remote(
            wmid.at[zs_of(q), t_xy], wfull.at[full_of(local, q), xy], ys, yr.at[q, y], at_plane(t_xy, t_y)
        )

    for step in NEAR_QUARTERS:
        q = (zq + step) % NQ
        landed(wmid.at[zs_of(q)], zr.at[q])
        plane(lambda t_xy, t_y: plane_copy(q, t_xy, t_y).start())
        pltpu.make_async_copy(wmid.at[zs_of(q), xy], wfull.at[full_of(local, q), xy], yr.at[q, y]).start()
    loads[2].wait()
    loads[3].wait()

    def core_copy(q, s):
        here = wfull.at[full_of(s * NC + c, q)]
        return remote(here, here, cs, cr.at[q, s], partner)

    def product(owner, q):
        start = pl.multiple_of(owner * block + q * part, part)
        return jnp.dot(
            tokens[:, pl.ds(start, part)], wfull[full_of(owner, q)].reshape(part, BLK),
            preferred_element_type=F32,
        )

    pre = jnp.zeros((tokens.shape[0], BLK), F32)
    for step in NEAR_QUARTERS:
        q = (zq + step) % NQ
        for d in (0, 1, 3, 2):
            s = (y + d) % NY
            mine = s * NC + c
            landed(wfull.at[full_of(mine, q)], yr.at[q, s])
            core_copy(q, s).start()
            pre += product(mine, q)
        for d in (0, 1, 3, 2):
            s = (y + d) % NY
            other = s * NC + 1 - c
            landed(wfull.at[full_of(other, q)], cr.at[q, s])
            pre += product(other, q)

    sig = jax.nn.sigmoid(pre)
    cot = cot_t[...].astype(F32).T
    grad_pre = (cot * sig * (1.0 + pre * (1.0 - sig))).astype(BF16)

    def term(owner, q):
        start = pl.multiple_of(owner * block + q * part, part)
        return lax.dot_general(
            tokens[:, pl.ds(start, part)], grad_pre, (((0,), (0,)), ((), ())),
            preferred_element_type=F32,
        )

    def pair_copy(q):
        return remote(psend.at[q], precv.at[q], ps, pr.at[q], partner)

    def back_copy(q, t_xy, t_y):
        return remote(
            ysend.at[q, t_y, :, t_xy], yrecv.at[q, y, :, xy], y2s, y2r.at[q, y], at_plane(t_xy, t_y)
        )

    for step in FAR_QUARTERS:
        q = (zq + step) % NQ
        for s in range(NY):
            psend[q, s] = term(s * NC + 1 - c, q)
        pair_copy(q).start()
    for step in FAR_QUARTERS:
        q = (zq + step) % NQ
        mine = [term(s * NC + c, q) for s in range(NY)]
        landed(precv.at[q], pr.at[q])
        for s in range(NY):
            ysend[q, s] = (mine[s] + precv[q, s]).astype(BF16).reshape(NQ, NXY, rows, BLK)
        plane(lambda t_xy, t_y: back_copy(q, t_xy, t_y).start())
        pltpu.make_async_copy(ysend.at[q, y, :, xy], yrecv.at[q, y, :, xy], y2r.at[q, y]).start()
    act_t[...] = (pre * sig).T.astype(BF16)
    act_copy = pltpu.make_async_copy(act_t, act_hbm, act_sem)
    act_copy.start()

    landed(wsend.at[:NZ - 1], zs)
    landed(wfull.at[:NQ * (NXY * NY - 1) // 2], ys)
    landed(wfull.at[:NZ * NY], cs)
    landed(psend, ps)

    def home_copy(t):
        return remote(gmid.at[t], glast.at[z], z2s, z2r, at_z(t))

    for step in FAR_QUARTERS:
        q = (zq + step) % NQ
        total = None
        for d in (0, 1, 3, 2):
            s = (y + d) % NY
            landed(yrecv.at[q, s], y2r.at[q, s])
            term_here = yrecv[q, s].reshape(part, BLK).astype(F32)
            total = term_here if total is None else total + term_here
        gmid[zs_of(q)] = (total * factor).astype(BF16).reshape(NQ, NXY, rows, BLK)
        for i in range(NQ):
            t = q * NQ + (i if step else (zi + i) % NQ)
            if step or i:
                home_copy(t).start()
    pltpu.make_async_copy(gmid.at[z], glast.at[z], z2r).start()
    act_copy.wait()
    landed(wfull.at[:NQ * (NXY * NY - 1) // 2], y2s)
    landed(gmid.at[:NZ - 1], z2s)
    landed(glast, z2r)


def finish(act_in, glast, act_t, grad_out):
    act_t[...] = act_in[...]
    for n in range(NZ * NXY):
        grad_out[:, n * BLK:(n + 1) * BLK] = glast[n // NXY, n % NXY]


def body(tokens, codes, scales, cotangent):
    tok_rows, depth = tokens.shape
    rows, width = codes.shape
    part = NQ * NXY * rows
    factor = (tok_rows * NY * NC) ** (-0.5)
    piece = (NZ, NXY, rows, BLK)
    dma = pltpu.SemaphoreType.DMA
    act_t, grad = pl.pallas_call(
        functools.partial(kernel, rows, factor),
        out_shape=(
            jax.ShapeDtypeStruct((BLK, tok_rows), BF16),
            jax.ShapeDtypeStruct(piece, BF16),
        ),
        in_specs=[pl.BlockSpec(memory_space=pl.ANY)] * 4,
        out_specs=(pl.BlockSpec(memory_space=pl.ANY),) * 2,
        scratch_shapes=[
            pltpu.VMEM((tok_rows, depth), BF16),
            pltpu.VMEM((rows, width), BF16),
            pltpu.VMEM(scales.shape, BF16),
            pltpu.VMEM((BLK, tok_rows), BF16),
            pltpu.VMEM((BLK, tok_rows), BF16),
            pltpu.VMEM(piece, BF16),
            pltpu.VMEM(piece, BF16),
            pltpu.VMEM((NY * NC * NZ, NXY, rows, BLK), BF16),
            pltpu.VMEM((NQ, NY, part, BLK), F32),
            pltpu.VMEM((NQ, NY, part, BLK), F32),
            pltpu.VMEM((NQ, NY, NQ, NXY, rows, BLK), BF16),
            pltpu.VMEM((NQ, NY, NQ, NXY, rows, BLK), BF16),
            pltpu.VMEM(piece, BF16),
            dma((4,)), dma, dma, dma((NQ,)), dma, dma((NQ, NY)), dma, dma((NQ, NY)),
            dma, dma((NQ,)), dma, dma((NQ, NY)), dma, dma,
        ],
        compiler_params=pltpu.CompilerParams(
            collective_id=0, has_side_effects=True, vmem_limit_bytes=62 << 20
        ),
        cost_estimate=pl.CostEstimate(
            flops=4 * tok_rows * depth * BLK, bytes_accessed=4 << 20, transcendentals=tok_rows * BLK
        ),
    )(tokens, codes, scales, cotangent.T)
    act_t, grad = pl.pallas_call(
        finish,
        out_shape=(
            jax.ShapeDtypeStruct((BLK, tok_rows), BF16),
            jax.ShapeDtypeStruct((rows, width), BF16),
        ),
        in_specs=[VMEM, VMEM],
        out_specs=(VMEM, VMEM),
    )(act_t, grad)
    return (act_t.T, grad)


def solution(mesh):
    placed = (
        P("local", None),
        P(("local", "node"), None),
        P(("local", "node"), None),
        P("local", "node"),
    )
    return jax.shard_map(
        body,
        mesh=mesh,
        in_specs=placed,
        out_specs=(P("local", "node"), P(("local", "node"), None)),
        check_vma=False,
    )
```

```python
import functools

import jax
import jax.numpy as jnp
from jax import lax
from jax.experimental import pallas as pl
from jax.experimental.pallas import tpu as pltpu
from jax.sharding import PartitionSpec as P

BLK = 112
MESH = pl.DeviceIdType.MESH
NZ, NXY, NY, NC = 16, 8, 4, 2
NQ = 4
NEAR_FIRST = (1, 15, 2, 14, 3, 13, 4, 12, 5, 11, 6, 10, 7, 9, 8)
NEAR_QUARTERS = (0, 1, 3, 2)
BACK_QUARTERS = (0, 1, 2, 3)
VMEM = pl.BlockSpec(memory_space=pltpu.VMEM)
F32, BF16 = jnp.float32, jnp.bfloat16


def kernel(
    rows, factor,
    tokens_hbm, codes_hbm, scales_hbm, cot_hbm,
    act_hbm, glast,
    tokens, codes, scales, cot_t, act_t,
    wsend, wmid, wfull, psend, precv, ysend, yrecv, gmid,
    in_sem, act_sem, zs, zr, ys, yr, cs, cr,
    ps, pr, y2s, y2r, z2s, z2r,
):
    node, local = lax.axis_index("node"), lax.axis_index("local")
    z, xy, y, c = node // NXY, node % NXY, local // NC, local % NC
    zq = z // NQ
    part = NQ * NXY * rows
    block = NQ * part
    partner = (node, y * NC + (1 - c))

    def at_z(other):
        return (other * NXY + xy, local)

    def at_plane(other_xy, other_y):
        return (z * NXY + other_xy, other_y * NC + c)

    def remote(src, dst, send_sem, recv_sem, device):
        return pltpu.make_async_remote_copy(
            src_ref=src, dst_ref=dst, send_sem=send_sem, recv_sem=recv_sem,
            device_id=device, device_id_type=MESH,
        )

    def landed(ref, sem):
        pltpu.make_async_copy(ref, ref, sem).wait()

    def plane(visit):
        for dy in (2, 1, 3, 0):
            @pl.loop(0 if dy else 1, NXY)
            def _(dx):
                visit((xy + dx) % NXY, (y + dy) % NY)

    loads = [
        pltpu.make_async_copy(src, dst, in_sem.at[i])
        for i, (src, dst) in enumerate(
            ((codes_hbm, codes), (scales_hbm, scales), (tokens_hbm, tokens), (cot_hbm, cot_t))
        )
    ]
    for load in loads:
        load.start()

    barrier = pltpu.get_barrier_semaphore()

    def greet(device):
        pl.semaphore_signal(barrier, inc=1, device_id=device, device_id_type=MESH)

    for d in NEAR_FIRST[::-1]:
        greet(at_z((z + d) % NZ))
    plane(lambda t_xy, t_y: greet(at_plane(t_xy, t_y)))
    greet(partner)

    loads[0].wait()
    loads[1].wait()

    scale = scales[...].astype(F32)
    for n in range(NZ * NXY):
        piece = codes[:, n * BLK:(n + 1) * BLK].astype(F32) * scale[:, n:n + 1]
        wsend[n // NXY, n % NXY] = piece.astype(BF16)

    pl.semaphore_wait(barrier, NZ - 1 + NXY * NY - 1 + 1)

    def z_copy(d):
        t = (z + d) % NZ
        return remote(wsend.at[t], wmid.at[z], zs, zr.at[zq], at_z(t))

    for d in NEAR_FIRST:
        z_copy(d).start()
    pltpu.make_async_copy(wsend.at[z], wmid.at[z], zr.at[zq]).start()

    def zs_of(q):
        return pl.ds(q * NQ, NQ)

    def full_of(owner, q):
        return pl.ds(owner * NZ + q * NQ, NQ)

    def plane_copy(q, t_xy, t_y):
        return remote(
            wmid.at[zs_of(q), t_xy], wfull.at[full_of(local, q), xy], ys, yr.at[q], at_plane(t_xy, t_y)
        )

    for step in NEAR_QUARTERS:
        q = (zq + step) % NQ
        landed(wmid.at[zs_of(q)], zr.at[q])
        plane(lambda t_xy, t_y: plane_copy(q, t_xy, t_y).start())
        pltpu.make_async_copy(wmid.at[zs_of(q), xy], wfull.at[full_of(local, q), xy], yr.at[q]).start()
    loads[2].wait()
    loads[3].wait()

    def core_copy(q, s):
        here = wfull.at[full_of(s * NC + c, q)]
        return remote(here, here, cs, cr.at[q, s], partner)

    def product(owner, q):
        start = pl.multiple_of(owner * block + q * part, part)
        return jnp.dot(
            tokens[:, pl.ds(start, part)], wfull[full_of(owner, q)].reshape(part, BLK),
            preferred_element_type=F32,
        )

    pre = jnp.zeros((tokens.shape[0], BLK), F32)
    for step in NEAR_QUARTERS:
        q = (zq + step) % NQ
        landed(wfull.at[:NZ], yr.at[q])
        for d in range(NY):
            core_copy(q, d).start()
        for d in (0, 1, 3, 2):
            s = (y + d) % NY
            mine = s * NC + c
            pre += product(mine, q)
        for d in (0, 1, 3, 2):
            s = (y + d) % NY
            other = s * NC + 1 - c
            landed(wfull.at[full_of(other, q)], cr.at[q, s])
            pre += product(other, q)

    sig = jax.nn.sigmoid(pre)
    cot = cot_t[...].astype(F32).T
    grad_pre = (cot * sig * (1.0 + pre * (1.0 - sig))).astype(BF16)

    def term(owner, q):
        start = pl.multiple_of(owner * block + q * part, part)
        return lax.dot_general(
            tokens[:, pl.ds(start, part)], grad_pre, (((0,), (0,)), ((), ())),
            preferred_element_type=F32,
        )

    def pair_copy(q):
        return remote(psend.at[q], precv.at[q], ps, pr.at[q], partner)

    def back_copy(q, t_xy, t_y):
        return remote(
            ysend.at[q, t_y, :, t_xy], yrecv.at[q, y, :, xy], y2s, y2r.at[q], at_plane(t_xy, t_y)
        )

    def to_pair(q):
        for s in range(NY):
            psend[q, s] = term(s * NC + 1 - c, q)
        pair_copy(q).start()

    def to_plane(q):
        mine = [term(s * NC + c, q) for s in range(NY)]
        landed(precv.at[q], pr.at[q])
        for s in range(NY):
            ysend[q, s] = (mine[s] + precv[q, s]).astype(BF16).reshape(NQ, NXY, rows, BLK)
        plane(lambda t_xy, t_y: back_copy(q, t_xy, t_y).start())
        pltpu.make_async_copy(ysend.at[q, y, :, xy], yrecv.at[q, y, :, xy], y2r.at[q]).start()

    to_pair(BACK_QUARTERS[0])
    to_pair(BACK_QUARTERS[1])
    to_plane(BACK_QUARTERS[0])
    to_pair(BACK_QUARTERS[2])
    to_plane(BACK_QUARTERS[1])
    to_pair(BACK_QUARTERS[3])
    to_plane(BACK_QUARTERS[2])
    to_plane(BACK_QUARTERS[3])
    act_t[...] = (pre * sig).T.astype(BF16)
    act_copy = pltpu.make_async_copy(act_t, act_hbm, act_sem)
    act_copy.start()

    landed(wsend.at[:NZ - 1], zs)
    landed(wfull.at[:NQ * (NXY * NY - 1) // 2], ys)
    landed(wfull.at[:NZ * NY], cs)
    landed(psend, ps)

    def home_copy(t):
        return remote(gmid.at[t], glast.at[z], z2s, z2r, at_z(t))

    for q in BACK_QUARTERS:
        landed(yrecv.at[q], y2r.at[q])
        total = None
        for d in (0, 1, 3, 2):
            s = (y + d) % NY
            term_here = yrecv[q, s].reshape(part, BLK).astype(F32)
            total = term_here if total is None else total + term_here
        gmid[zs_of(q)] = (total * factor).astype(BF16).reshape(NQ, NXY, rows, BLK)
        for i in range(NQ):
            t = q * NQ + i

            @pl.when(t != z)
            def _():
                home_copy(t).start()

    pltpu.make_async_copy(gmid.at[z], glast.at[z], z2r).start()
    act_copy.wait()
    landed(wfull.at[:NQ * (NXY * NY - 1) // 2], y2s)
    landed(gmid.at[:NZ - 1], z2s)
    landed(glast, z2r)


def finish(act_in, glast, act_t, grad_out):
    act_t[...] = act_in[...]
    for n in range(NZ * NXY):
        grad_out[:, n * BLK:(n + 1) * BLK] = glast[n // NXY, n % NXY]


def body(tokens, codes, scales, cotangent):
    tok_rows, depth = tokens.shape
    rows, width = codes.shape
    part = NQ * NXY * rows
    factor = (tok_rows * NY * NC) ** (-0.5)
    piece = (NZ, NXY, rows, BLK)
    dma = pltpu.SemaphoreType.DMA
    act_t, grad = pl.pallas_call(
        functools.partial(kernel, rows, factor),
        out_shape=(
            jax.ShapeDtypeStruct((BLK, tok_rows), BF16),
            jax.ShapeDtypeStruct(piece, BF16),
        ),
        in_specs=[pl.BlockSpec(memory_space=pl.ANY)] * 4,
        out_specs=(pl.BlockSpec(memory_space=pl.ANY),) * 2,
        scratch_shapes=[
            pltpu.VMEM((tok_rows, depth), BF16),
            pltpu.VMEM((rows, width), BF16),
            pltpu.VMEM(scales.shape, BF16),
            pltpu.VMEM((BLK, tok_rows), BF16),
            pltpu.VMEM((BLK, tok_rows), BF16),
            pltpu.VMEM(piece, BF16),
            pltpu.VMEM(piece, BF16),
            pltpu.VMEM((NY * NC * NZ, NXY, rows, BLK), BF16),
            pltpu.VMEM((NQ, NY, part, BLK), F32),
            pltpu.VMEM((NQ, NY, part, BLK), F32),
            pltpu.VMEM((NQ, NY, NQ, NXY, rows, BLK), BF16),
            pltpu.VMEM((NQ, NY, NQ, NXY, rows, BLK), BF16),
            pltpu.VMEM(piece, BF16),
            dma((4,)), dma, dma, dma((NQ,)), dma, dma((NQ,)), dma, dma((NQ, NY)),
            dma, dma((NQ,)), dma, dma((NQ,)), dma, dma,
        ],
        compiler_params=pltpu.CompilerParams(
            collective_id=0, has_side_effects=True, vmem_limit_bytes=62 << 20
        ),
        cost_estimate=pl.CostEstimate(
            flops=4 * tok_rows * depth * BLK, bytes_accessed=4 << 20, transcendentals=tok_rows * BLK
        ),
    )(tokens, codes, scales, cotangent.T)
    act_t, grad = pl.pallas_call(
        finish,
        out_shape=(
            jax.ShapeDtypeStruct((BLK, tok_rows), BF16),
            jax.ShapeDtypeStruct((rows, width), BF16),
        ),
        in_specs=[VMEM, VMEM],
        out_specs=(VMEM, VMEM),
    )(act_t, grad)
    return (act_t.T, grad)


def solution(mesh):
    placed = (
        P("local", None),
        P(("local", "node"), None),
        P(("local", "node"), None),
        P("local", "node"),
    )
    return jax.shard_map(
        body,
        mesh=mesh,
        in_specs=placed,
        out_specs=(P("local", "node"), P(("local", "node"), None)),
        check_vma=False,
    )
```
